32 devices in a mesh: req: 8 (over z, y), head: 4 (over x, core).
Axes of the slice: x: 2, y: 2, z: 4, core: 2. Of those that a mesh axis runs over, the one named last changes fastest.
Arguments:
- queries: bfloat16 [16, 512, 4096], P('req', None, 'head'), may hold values from -16 to 16
- new_keys: bfloat16 [16, 512, 1024], P('req', None, 'head'), may hold values from -16 to 16
- incoming_values: bfloat16 [16, 512, 1024], P('req', None, 'head'), may hold values from -6 to 6
- request_cached_keys: bfloat16 [16, 2048, 1024], P('req', None, 'head'), may hold values from -12 to 12
- request_cached_values: bfloat16 [16, 2048, 1024], P('req', None, 'head'), may hold values from -6 to 6
- cache_lengths: int32 [16], P('req'), may hold values from 1 to 2048, 16384 in all
- out_weight: bfloat16 [4096, 4096], P('head'), may hold values from -0.25 to 0.25
- residual: bfloat16 [512, 16, 4096], P(('req', 'head')), may hold values from -3 to 3
- norm_gain: bfloat16 [4096], replicated, may hold values from 0.5 to 1.5
Outputs:
- hidden: bfloat16 [512, 16, 4096], P(('req', 'head'))
- normed: bfloat16 [512, 16, 4096], P(('req', 'head'))
The draws below stay inside these ranges and needn't reach their ends.
Inputs may be any that keep to these rules, and one draw needn't show every extreme that they name: Request r's cache holds keys in slots 0 to cache_lengths[r] - 1; in every draw the longest request has exactly 2048.
All inputs are finite; a program needn't handle non-finite values. No bound on the sum of `cache_lengths` on one device may be relied on, other than what follows from the above.
Results may differ from the reference program's by a relative error of at most 0.013.
Values may be sent and summed in bfloat16 or wider, within the bound.
No kernel may reach another device: no remote copies, remote signals or barrier semaphores. Data moves between devices by JAX's collectives and lax.ppermute only.
A program may use at most 128 MiB of HBM per device.

```python
import math
import jax
import jax.numpy as jnp
import numpy as np
from jax import lax

D = 4096
QUERY_HEADS = 32
KEY_VALUE_HEADS = 8
HEAD_SIZE = 128
NEW_TOKEN_COUNT = 512
CACHE_SLOTS = 2048
REQUEST_TOTAL = 16
N_HEAD = 4


def draw_queries(key, part):
    gaussian_sample = jax.random.normal(jax.random.fold_in(key, 1), (REQUEST_TOTAL, NEW_TOKEN_COUNT, QUERY_HEADS * HEAD_SIZE), jnp.float32)
    gaussian_sample = jnp.clip(gaussian_sample, -6.0, 6.0)
    return gaussian_sample.astype(jnp.bfloat16)


def draw_new_keys(key, part):
    gaussian_sample = 2.0 * jax.random.normal(jax.random.fold_in(key, 2), (REQUEST_TOTAL, NEW_TOKEN_COUNT, KEY_VALUE_HEADS * HEAD_SIZE), jnp.float32)
    gaussian_sample = jnp.clip(gaussian_sample, -12.0, 12.0)
    return gaussian_sample.astype(jnp.bfloat16)


def shard_levels(rng, shape, pieces, low, top_value):
    def one(dim, shards_of):
        heights = jax.random.uniform(jax.random.fold_in(jax.random.fold_in(rng, 6), dim), (shards_of,), jnp.float32, low / len(pieces), top_value / len(pieces))
        return jnp.repeat(jnp.exp(heights), shape[dim] // shards_of).reshape((-1,) + (1,) * (len(shape) - dim - 1))

    level = one(*pieces[0])
    for cut in pieces[1:]:
        level = level * one(*cut)
    return level


def profile(amount, total, most, slope):
    portions = [(1 << 20) // math.isqrt(rank ** slope) + 1 for rank in range(2, amount + 1)]
    rest, counts = total - most - (amount - 1), [1] * (amount - 1)
    while rest > 0:
        movable = [i for i in range(amount - 1) if counts[i] < most]
        whole, budget = sum([portions[i] for i in movable]), rest
        for i in movable:
            extra = min(most - counts[i], max(1, budget * portions[i] // whole), rest)
            counts[i] = counts[i] + extra
            rest = rest - extra
    return np.array([most] + counts)


def uneven_parts(key, count, total, limit, skew):
    if count == 2:
        one = jax.random.randint(key, (), max(1, total - limit), min(limit, total - 1) + 1)
        return jnp.stack([one, total - one])
    sizes = jnp.asarray(profile(count, total, limit, skew), jnp.int32)
    couples = (count - 1) // 2
    giver, receiver = sizes[1:1 + 2 * couples:2], sizes[2:2 + 2 * couples:2]
    slack = jnp.minimum(giver - 1, limit - receiver)
    shifted = jax.random.randint(jax.random.fold_in(key, 1), (couples,), 0, 1 << 20) % (slack + 1)
    sizes = sizes.at[1:1 + 2 * couples:2].set(giver - shifted).at[2:2 + 2 * couples:2].set(receiver + shifted)
    return sizes[jax.random.permutation(jax.random.fold_in(key, 2), count)]


def centred(own_key, shape, spread, most, split=(), kind=jnp.bfloat16):
    values = spread * jax.random.normal(own_key, shape, jnp.float32)
    if split:
        values = values * shard_levels(own_key, shape, split, -0.22, 0.18)
    return jnp.clip(values, -most, most).astype(kind)


def setup_inputs(seed: int = 0) -> dict:
    splits = jax.random.split(jax.random.key(seed), 10)
    queries = draw_queries(jax.random.fold_in(splits[9], 71), 0)
    new_keys = draw_new_keys(jax.random.fold_in(splits[9], 71), 0)
    incoming_values = centred(splits[2], (REQUEST_TOTAL, NEW_TOKEN_COUNT, KEY_VALUE_HEADS * HEAD_SIZE), 1.0, 6.0, ((0, 8), (2, 4)))
    request_cached_keys = centred(splits[3], (REQUEST_TOTAL, CACHE_SLOTS, KEY_VALUE_HEADS * HEAD_SIZE), 2.0, 12.0, ((0, 8), (2, 4)))
    request_cached_values = centred(splits[4], (REQUEST_TOTAL, CACHE_SLOTS, KEY_VALUE_HEADS * HEAD_SIZE), 1.0, 6.0, ((0, 8), (2, 4)))
    cache_lengths = uneven_parts(splits[5], REQUEST_TOTAL, REQUEST_TOTAL * CACHE_SLOTS // 2, CACHE_SLOTS, 2).astype(jnp.int32)
    out_weight = centred(splits[6], (QUERY_HEADS * HEAD_SIZE, D), (QUERY_HEADS * HEAD_SIZE // 8) ** -0.5, 0.25, ((0, 4),))
    residual = centred(splits[7], (NEW_TOKEN_COUNT, REQUEST_TOTAL, D), 0.5, 3.0, ((0, 32),))
    norm_gain = jnp.clip(1.0 + 0.1 * jax.random.normal(splits[8], (D,), jnp.float32), 0.5, 1.5).astype(jnp.bfloat16)
    return dict(queries=queries, new_keys=new_keys, incoming_values=incoming_values, request_cached_keys=request_cached_keys, request_cached_values=request_cached_values, cache_lengths=cache_lengths, out_weight=out_weight, residual=residual, norm_gain=norm_gain)


NEGATIVE_FILLER = -1e+30

def soak_into(carried_along, query_head_count, key_row_block, value_row_block, visible, logit_scale):
    running_max, running_sum, running_out = carried_along
    scores = jnp.einsum('qgjd,kgd->gjqk', query_head_count.astype(jnp.float32), key_row_block.astype(jnp.float32)) * logit_scale
    scores = jnp.where(visible, scores, NEGATIVE_FILLER)
    new_max = jnp.maximum(running_max, lax.optimization_barrier(jnp.max(scores, axis=-1)))
    rescale = jnp.exp(running_max - new_max)
    weights = jnp.exp(scores - new_max[..., None])
    running_sum = running_sum * rescale + lax.optimization_barrier(jnp.sum(weights, axis=-1))
    rounded = lax.optimization_barrier(weights.astype(jnp.bfloat16)).astype(jnp.float32)
    running_out = running_out * rescale[..., None] + jnp.einsum('gjqk,kgd->gjqd', rounded, value_row_block.astype(jnp.float32))
    return (new_max, running_sum, running_out)

def attend_one(query_row_block, incoming_key, incoming_value, stored_key_cache, stored_value_cache, length):
    group_members = QUERY_HEADS // KEY_VALUE_HEADS
    query_head_count = query_row_block.reshape(NEW_TOKEN_COUNT, KEY_VALUE_HEADS, group_members, HEAD_SIZE)
    logit_scale = 1.0 / math.sqrt(HEAD_SIZE)
    block_extent = min(512, CACHE_SLOTS)
    carried_along = (jnp.full((KEY_VALUE_HEADS, group_members, NEW_TOKEN_COUNT), NEGATIVE_FILLER, jnp.float32), jnp.zeros((KEY_VALUE_HEADS, group_members, NEW_TOKEN_COUNT), jnp.float32), jnp.zeros((KEY_VALUE_HEADS, group_members, NEW_TOKEN_COUNT, HEAD_SIZE), jnp.float32))
    block_count = (length + block_extent - 1) // block_extent

    def cache_step(block_id, carried_along):
        start_shift = (block_id * block_extent).astype(jnp.int32)
        key_row_block = lax.dynamic_slice_in_dim(stored_key_cache, start_shift, block_extent, 0).reshape(block_extent, KEY_VALUE_HEADS, HEAD_SIZE)
        value_row_block = lax.dynamic_slice_in_dim(stored_value_cache, start_shift, block_extent, 0).reshape(block_extent, KEY_VALUE_HEADS, HEAD_SIZE)
        positions = start_shift + jnp.arange(block_extent, dtype=jnp.int32)
        visible = (positions < length)[None, None, None, :]
        return soak_into(carried_along, query_head_count, key_row_block, value_row_block, visible, logit_scale)
    carried_along = lax.fori_loop(0, block_count, cache_step, carried_along)
    row_index = jnp.arange(NEW_TOKEN_COUNT, dtype=jnp.int32)
    causal_mask = (row_index[None, :] <= row_index[:, None])[None, None, :, :]
    carried_along = soak_into(carried_along, query_head_count, incoming_key.reshape(NEW_TOKEN_COUNT, KEY_VALUE_HEADS, HEAD_SIZE), incoming_value.reshape(NEW_TOKEN_COUNT, KEY_VALUE_HEADS, HEAD_SIZE), causal_mask, logit_scale)
    running_max, running_sum, running_out = carried_along
    finished = running_out / running_sum[..., None]
    return finished.transpose(2, 0, 1, 3).reshape(NEW_TOKEN_COUNT, QUERY_HEADS * HEAD_SIZE).astype(jnp.bfloat16)

def reference(queries, new_keys, incoming_values, request_cached_keys, request_cached_values, cache_lengths, out_weight, residual, norm_gain):
    attended = lax.map(lambda packed: attend_one(*packed), (queries, new_keys, incoming_values, request_cached_keys, request_cached_values, cache_lengths))
    flat_rows = attended.reshape(REQUEST_TOTAL * NEW_TOKEN_COUNT, QUERY_HEADS * HEAD_SIZE)
    group_width = QUERY_HEADS * HEAD_SIZE // N_HEAD
    accumulated = jnp.zeros((REQUEST_TOTAL * NEW_TOKEN_COUNT, D), jnp.float32)
    for group_id in range(N_HEAD):
        partial_term = jnp.dot(flat_rows[:, group_id * group_width:(group_id + 1) * group_width], out_weight[group_id * group_width:(group_id + 1) * group_width], preferred_element_type=jnp.float32)
        accumulated = accumulated + lax.optimization_barrier(partial_term.astype(jnp.bfloat16)).astype(jnp.float32)
    attn_out = accumulated.astype(jnp.bfloat16).reshape(REQUEST_TOTAL, NEW_TOKEN_COUNT, D).transpose(1, 0, 2)
    summed = residual.astype(jnp.float32) + lax.optimization_barrier(attn_out).astype(jnp.float32)
    hidden = summed.astype(jnp.bfloat16)
    mean_square = lax.optimization_barrier(jnp.mean(summed * summed, axis=-1, keepdims=True))
    normed = (summed * lax.rsqrt(mean_square + 1e-05) * norm_gain.astype(jnp.float32)).astype(jnp.bfloat16)
    return (hidden, normed)
```

```python
import functools
import math

import jax
import jax.numpy as jnp
from jax import lax
from jax.experimental import pallas as pl
from jax.experimental.pallas import tpu as pltpu
from jax.sharding import Mesh, PartitionSpec as P

QUERY_HEADS = 32
KEY_VALUE_HEADS = 8
HEAD_SIZE = 128
MEMBERS = QUERY_HEADS // KEY_VALUE_HEADS
NEGATIVE_FILLER = -1e30
EXPONENT_SCALE = math.log2(math.e) / math.sqrt(HEAD_SIZE)
CONTRACT_LAST = (((1,), (1,)), ((), ()))
MIB = 2**20
SIDE_IN_QUERIES, SIDE, CORE = -3, -2, -1


def in_hbm(array):
    return pltpu.with_memory_space_constraint(array, pltpu.HBM)


def resident(array):
    return pltpu.with_memory_space_constraint(array, pltpu.VMEM)


def scalar(facts_ref, which):
    return facts_ref[facts_ref.shape[0] + which]


def with_ones(values):
    return jnp.concatenate([values, jnp.ones((values.shape[0], HEAD_SIZE), jnp.bfloat16)], axis=1)


def weights_of(scores, row_max):
    tiled = jnp.concatenate([row_max] * (scores.shape[1] // HEAD_SIZE), axis=1)
    return jnp.exp2((scores - tiled) * EXPONENT_SCALE).astype(jnp.bfloat16)


class Projection:
    def __init__(self, facts_ref, sources, parts, weights, scratch):
        self.sources = sources
        self.weights = weights
        self.parts_ref, self.lhs_ref, self.w_ref, self.parts_sem, self.w_sem = scratch
        core = scalar(facts_ref, CORE)
        self.part_copies = [
            pltpu.make_async_copy(
                part.at[:, core if k == 0 else 1 - core],
                self.parts_ref.at[k, n],
                self.parts_sem.at[k, n],
            )
            for k in range(2)
            for n, part in enumerate(parts)
        ]

    @staticmethod
    def scratch(count, part, weight):
        sources, _, rows, depth = part.shape
        columns = weight.shape[1]
        block = min(512, columns)
        return [
            pltpu.VMEM((2, count, sources, rows, depth), jnp.bfloat16),
            pltpu.VMEM((2, count * sources * rows, depth), jnp.bfloat16),
            pltpu.VMEM((2, columns // block, depth, block), jnp.bfloat16),
            pltpu.SemaphoreType.DMA((2, count)),
            pltpu.SemaphoreType.DMA((2, columns // block)),
        ]

    def weight_copy(self, k, n):
        block = self.w_ref.shape[3]
        return pltpu.make_async_copy(
            self.weights[k].at[:, pl.ds(n * block, block)],
            self.w_ref.at[k, n],
            self.w_sem.at[k, n],
        )

    def start_parts(self):
        for copy in self.part_copies:
            copy.start()

    def start_block(self, n):
        if n < self.w_ref.shape[1]:
            for k in range(2):
                self.weight_copy(k, n).start()

    def arrange(self):
        _, count, sources, rows, depth = self.parts_ref.shape
        size = sources * rows
        target = lax.broadcasted_iota(jnp.int32, (size, size), 0)
        origin = lax.broadcasted_iota(jnp.int32, (size, size), 1)
        wanted = target % self.sources * (size // self.sources) + target // self.sources
        order = jnp.where(origin == wanted, 1.0, 0.0).astype(jnp.bfloat16)
        for copy in self.part_copies:
            copy.wait()
        for k in range(2):
            for n in range(count):
                self.lhs_ref[k, n * size : (n + 1) * size] = jnp.dot(
                    order,
                    self.parts_ref[k, n].reshape(size, depth),
                    preferred_element_type=jnp.float32,
                ).astype(jnp.bfloat16)

    def column_block(self, n):
        for k in range(2):
            self.weight_copy(k, n).wait()
        return jnp.dot(
            self.lhs_ref[0], self.w_ref[0, n], preferred_element_type=jnp.float32
        ) + jnp.dot(self.lhs_ref[1], self.w_ref[1, n], preferred_element_type=jnp.float32)


def attention_kernel(
    request, span, stride, sources, facts_ref, q_hbm, nk_hbm, nv_hbm, ck_hbm, cv_hbm, *refs
):
    projecting = len(refs) > 12
    if projecting:
        parts_any, w_mine_hbm, w_other_hbm, out_hbm, partial_hbm, *refs = refs
    else:
        out_hbm, *refs = refs
    q_ref, nk_ref, nv_ref, ck_ref, cv_ref, max_ref, acc_ref, done_ref = refs[:8]
    new_sem, cache_sem, out_sem = refs[8:11]
    kv_local, rows = nk_ref.shape[1] // HEAD_SIZE, max_ref.shape[1]
    new_count, slots = nk_ref.shape[0], ck_ref.shape[0]
    small = min(512, slots)
    length = facts_ref[request]
    first = scalar(facts_ref, SIDE) * span

    new_copies = [
        pltpu.make_async_copy(
            q_hbm.at[request, :, scalar(facts_ref, SIDE_IN_QUERIES)], q_ref, new_sem.at[0]
        ),
        pltpu.make_async_copy(nk_hbm.at[request], nk_ref, new_sem.at[1]),
        pltpu.make_async_copy(nv_hbm.at[request], nv_ref, new_sem.at[2]),
    ]

    def cache_copies(block):
        part = pl.ds(pl.multiple_of(block * small, small), small)
        return (
            pltpu.make_async_copy(
                ck_hbm.at[request, part], ck_ref.at[part], cache_sem.at[0, block]
            ),
            pltpu.make_async_copy(
                cv_hbm.at[request, part], cv_ref.at[part], cache_sem.at[1, block]
            ),
        )

    for copy in new_copies:
        copy.start()
    for block in range(slots // small):

        @pl.when(block * small < length)
        def _(block=block):
            for copy in cache_copies(block):
                copy.start()

    def absorb(g, keys, values, mask, fresh):
        def product(h):
            low = (g * MEMBERS + h) * HEAD_SIZE
            return lax.dot_general(
                q_ref[:, :, low : low + HEAD_SIZE].reshape(rows, HEAD_SIZE),
                keys,
                CONTRACT_LAST,
                preferred_element_type=jnp.float32,
            )

        scores = product(0)
        for h in range(MEMBERS):
            index = g * MEMBERS + h
            following = product(h + 1) if h + 1 < MEMBERS else None
            if mask is not None:
                scores = jnp.where(mask, scores, NEGATIVE_FILLER)
            block_max = jnp.max(scores, axis=1, keepdims=True)
            if fresh:
                new_max = jnp.broadcast_to(block_max, (rows, HEAD_SIZE))
                weights = weights_of(scores, new_max)
                acc_ref[index] = jnp.dot(weights, values, preferred_element_type=jnp.float32)
            else:
                old_max = max_ref[index]
                new_max = jnp.maximum(old_max, block_max)
                rescale = jnp.exp2((old_max - new_max) * EXPONENT_SCALE)
                weights = weights_of(scores, new_max)
                acc_ref[index] = acc_ref[index] * jnp.concatenate(
                    [rescale, rescale], axis=1
                ) + jnp.dot(weights, values, preferred_element_type=jnp.float32)
            max_ref[index] = new_max
            scores = following

    for copy in new_copies:
        copy.wait()
    row = lax.broadcasted_iota(jnp.int32, (rows, 1), 0)
    position = row // span * stride + first + row % span
    visible = lax.broadcasted_iota(jnp.int32, (rows, new_count), 1) <= position
    for g in range(kv_local):
        lanes = slice(g * HEAD_SIZE, (g + 1) * HEAD_SIZE)
        absorb(g, nk_ref[:, lanes], with_ones(nv_ref[:, lanes]), visible, True)
    if projecting:
        stage_ref, stage_sem = refs[11:13]
        projection = Projection(
            facts_ref, sources, [parts_any], (w_mine_hbm, w_other_hbm), refs[13:]
        )
        projection.start_parts()
        for n in range(projection.w_ref.shape[1]):
            projection.start_block(n)

    def cache_block(start, extent, masked):
        for block in range(extent // small):
            for copy in cache_copies(start // small + block):
                copy.wait()
        mask = None
        if masked:
            mask = lax.broadcasted_iota(jnp.int32, (1, extent), 1) < length - start
        for g in range(kv_local):
            lanes = slice(g * HEAD_SIZE, (g + 1) * HEAD_SIZE)
            absorb(
                g,
                ck_ref[pl.ds(start, extent), lanes],
                with_ones(cv_ref[pl.ds(start, extent), lanes]),
                mask,
                False,
            )

    start, extent = jnp.int32(0), slots
    while extent >= small:
        fits = length - start >= extent

        @pl.when(fits)
        def _(start=start, extent=extent):
            cache_block(pl.multiple_of(start, small), extent, False)

        start = jnp.where(fits, start + extent, start)
        extent //= 2

    @pl.when(start < length)
    def _():
        cache_block(pl.multiple_of(start, small), small, True)

    group = MEMBERS * HEAD_SIZE
    out_copies = []
    for g in range(kv_local):
        for index in range(g * MEMBERS, (g + 1) * MEMBERS):
            total = acc_ref[index]
            done_ref[:, index * HEAD_SIZE : (index + 1) * HEAD_SIZE] = (
                total[:, :HEAD_SIZE] / total[:, HEAD_SIZE:]
            ).astype(jnp.bfloat16)
        lanes = pl.ds(g * group, group)
        out_copies.append(
            pltpu.make_async_copy(done_ref.at[:, lanes], out_hbm.at[:, lanes], out_sem.at[g])
        )
        out_copies[-1].start()
    if projecting:
        projection.arrange()
        block = projection.w_ref.shape[3]
        for n in range(projection.w_ref.shape[1]):
            lanes = pl.ds(n * block, block)
            stage_ref[:, n * block : (n + 1) * block] = projection.column_block(n).astype(
                jnp.bfloat16
            )
            out_copies.append(
                pltpu.make_async_copy(
                    stage_ref.at[:, lanes], partial_hbm.at[:, lanes], stage_sem.at[n]
                )
            )
            out_copies[-1].start()
    for copy in out_copies:
        copy.wait()


def attend(request, span, stride, sources, facts, q, nk, nv, ck, cv, moved=None, weights=()):
    _, blocks, _, q_span, width = q.shape
    rows = blocks * q_span
    new_count, slots, kv_width = nk.shape[1], ck.shape[1], nk.shape[2]
    small = min(512, slots)
    in_place = pl.BlockSpec(memory_space=pltpu.HBM)
    out_specs = [in_place]
    out_shape = [pltpu.HBM((rows, width), jnp.bfloat16)]
    heads = width // HEAD_SIZE
    scratch = [
        pltpu.VMEM((blocks, q_span, width), jnp.bfloat16),
        pltpu.VMEM((new_count, kv_width), jnp.bfloat16),
        pltpu.VMEM((new_count, kv_width), jnp.bfloat16),
        pltpu.VMEM((slots, kv_width), jnp.bfloat16),
        pltpu.VMEM((slots, kv_width), jnp.bfloat16),
        pltpu.VMEM((heads, rows, HEAD_SIZE), jnp.float32),
        pltpu.VMEM((heads, rows, 2 * HEAD_SIZE), jnp.float32),
        pltpu.VMEM((rows, width), jnp.bfloat16),
        pltpu.SemaphoreType.DMA((3,)),
        pltpu.SemaphoreType.DMA((2, slots // small)),
        pltpu.SemaphoreType.DMA((kv_width // HEAD_SIZE,)),
    ]
    operands = [in_hbm(a) for a in (q, nk, nv, ck, cv)]
    if moved is not None:
        columns = weights[0].shape[1]
        out_rows = moved.shape[0] * moved.shape[2]
        operands += [in_hbm(moved)] + [in_hbm(w) for w in weights]
        out_specs.append(in_place)
        out_shape.append(pltpu.HBM((out_rows, columns), jnp.bfloat16))
        projection = Projection.scratch(1, moved, weights[0])
        scratch.append(pltpu.VMEM((out_rows, columns), jnp.bfloat16))
        scratch.append(pltpu.SemaphoreType.DMA((projection[2].shape[1],)))
        scratch += projection
    out = pl.pallas_call(
        functools.partial(attention_kernel, request, span, stride, sources),
        in_specs=[pl.BlockSpec(memory_space=pltpu.SMEM)] + [in_place] * len(operands),
        out_specs=out_specs,
        scratch_shapes=scratch,
        out_shape=out_shape,
        compiler_params=pltpu.CompilerParams(vmem_limit_bytes=48 * MIB),
        name="attend",
    )(facts, *operands)
    return out if moved is not None else (out[0], None)


def final_kernel(local, remote, sources, facts_ref, *refs):
    own, refs = refs[:local], refs[local:]
    w_mine_hbm, w_other_hbm, refs = refs[0], refs[1], refs[2:]
    arrived, refs = refs[: remote * local], refs[remote * local :]
    residual_hbm, gain_ref, hidden_hbm, normed_hbm, *refs = refs
    arrived_ref, residual_ref, hidden_ref, normed_ref, rows_ref, square_ref = refs[:6]
    arrived_sem, residual_sem, hidden_sem, normed_sem = refs[6:10]
    projection = Projection(facts_ref, sources, own, (w_mine_hbm, w_other_hbm), refs[10:])
    blocks, pieces, requests, block = residual_ref.shape
    rows = pieces * requests
    each = rows // local

    def lanes(n):
        return pl.ds(n * block, block)

    def block_copies(n):
        copies = [
            pltpu.make_async_copy(
                residual_hbm.at[:, :, lanes(n)], residual_ref.at[n], residual_sem.at[n]
            )
        ]
        for index, part in enumerate(arrived):
            copies.append(
                pltpu.make_async_copy(
                    part.at[:, lanes(n)], arrived_ref.at[index, n], arrived_sem.at[index, n]
                )
            )
        return copies

    def start_block(n):
        projection.start_block(n)
        if n < blocks:
            for copy in block_copies(n):
                copy.start()

    ahead = 3
    projection.start_parts()
    for n in range(ahead):
        start_block(n)
    projection.arrange()
    out_copies = []
    parts = block // HEAD_SIZE
    square_ref[...] = jnp.zeros_like(square_ref)
    for n in range(blocks):
        start_block(n + ahead)
        total = projection.column_block(n)
        for copy in block_copies(n):
            copy.wait()
        for request in range(local):
            mine = total[request * each : (request + 1) * each]
            for index in range(remote):
                mine += arrived_ref[index * local + request, n].astype(jnp.float32)
            for p in range(parts):
                rows_ref[n * parts + p, pl.ds(request, each, stride=local), :] = mine[
                    :, p * HEAD_SIZE : (p + 1) * HEAD_SIZE
                ]
        square = square_ref[...]
        for p in range(parts):
            span = slice(p * HEAD_SIZE, (p + 1) * HEAD_SIZE)
            value = rows_ref[n * parts + p] + residual_ref[n, :, :, span].reshape(
                rows, HEAD_SIZE
            ).astype(jnp.float32)
            hidden_ref[n, :, :, span] = value.reshape(pieces, requests, HEAD_SIZE).astype(
                jnp.bfloat16
            )
            rows_ref[n * parts + p] = value
            square += value * value
        square_ref[...] = square
        out_copies.append(
            pltpu.make_async_copy(
                hidden_ref.at[n], hidden_hbm.at[:, :, lanes(n)], hidden_sem.at[n]
            )
        )
        out_copies[-1].start()
    mean = jnp.sum(square_ref[...], axis=1, keepdims=True) * (1.0 / (blocks * block))
    scale = jnp.broadcast_to(lax.rsqrt(mean + 1e-05), (rows, HEAD_SIZE))
    for n in range(blocks):
        for p in range(parts):
            span = slice(p * HEAD_SIZE, (p + 1) * HEAD_SIZE)
            low = n * block + p * HEAD_SIZE
            gain = gain_ref[:, low : low + HEAD_SIZE].astype(jnp.float32)
            normed_ref[n, :, :, span] = (
                (rows_ref[n * parts + p] * scale * gain)
                .reshape(pieces, requests, HEAD_SIZE)
                .astype(jnp.bfloat16)
            )
        out_copies.append(
            pltpu.make_async_copy(
                normed_ref.at[n], normed_hbm.at[:, :, lanes(n)], normed_sem.at[n]
            )
        )
        out_copies[-1].start()
    for copy in out_copies:
        copy.wait()


def finish(facts, own, weights, arrived, sources, residual, gain):
    local, remote = len(own), len(arrived) // len(own)
    pieces, requests, columns = residual.shape
    rows = pieces * requests
    block = min(512, columns)
    count = columns // block
    in_place = pl.BlockSpec(memory_space=pltpu.HBM)
    shape = pltpu.HBM(residual.shape, jnp.bfloat16)
    operands = [in_hbm(a) for a in (*own, *weights, *arrived, residual)]
    stream = pltpu.VMEM((count, pieces, requests, block), jnp.bfloat16)
    return pl.pallas_call(
        functools.partial(final_kernel, local, remote, sources),
        in_specs=[pl.BlockSpec(memory_space=pltpu.SMEM)]
        + [in_place] * len(operands)
        + [pl.BlockSpec(memory_space=pltpu.VMEM)],
        out_specs=[in_place, in_place],
        scratch_shapes=[
            pltpu.VMEM((len(arrived), count, rows // local, block), jnp.bfloat16),
            stream,
            stream,
            stream,
            pltpu.VMEM((columns // HEAD_SIZE, rows, HEAD_SIZE), jnp.float32),
            pltpu.VMEM((rows, HEAD_SIZE), jnp.float32),
            pltpu.SemaphoreType.DMA((len(arrived), count)),
            pltpu.SemaphoreType.DMA((count,)),
            pltpu.SemaphoreType.DMA((count,)),
            pltpu.SemaphoreType.DMA((count,)),
        ]
        + Projection.scratch(local, own[0], weights[0]),
        out_shape=[shape, shape],
        compiler_params=pltpu.CompilerParams(vmem_limit_bytes=52 * MIB),
        name="finish",
    )(facts, *operands, gain.reshape(1, columns))


def after(array, *others):
    return lax.optimization_barrier((array,) + others)[0]


def body(
    queries,
    new_keys,
    incoming_values,
    request_cached_keys,
    request_cached_values,
    cache_lengths,
    out_weight,
    residual,
    norm_gain,
):
    local, new_count, width = queries.shape
    req_count, sides, cores = (lax.axis_size(a) for a in ("req", "hx", "hc"))
    piece = new_count // (req_count * sides * cores)
    span, stride = cores * piece, sides * cores * piece
    my_side, core = (lax.axis_index(a).astype(jnp.int32) for a in ("hx", "hc"))
    whole_tiles = piece % 16 == 0
    by_side = queries.reshape(local, req_count, sides, span, width)
    weights = (out_weight, lax.ppermute(out_weight, "hc", [(0, 1), (1, 0)]))

    def facts_of(shift):
        side = lax.rem(my_side + shift, sides)
        q, pick = by_side, side
        if not whole_tiles:
            q = lax.dynamic_index_in_dim(by_side, side, 2, keepdims=False)
            q, pick = q.reshape(local, 1, 1, req_count * span, width), jnp.zeros((), jnp.int32)
        return q, jnp.concatenate([cache_lengths, jnp.stack([pick, side, core])])

    chunks = {shift: facts_of(shift) for shift in range(sides)}

    def attended(request, shift, wait, moved=None):
        q, facts = chunks[shift]
        return attend(
            request,
            span,
            stride,
            req_count,
            after(facts, *wait),
            q,
            new_keys,
            incoming_values,
            request_cached_keys,
            request_cached_values,
            moved,
            weights,
        )

    def move(rows):
        moved = lax.all_to_all(rows, ("req", "hc"), 0, 0, tiled=True)
        moved = moved.reshape(req_count, cores, piece, width)
        if not whole_tiles:
            moved = moved.transpose(1, 0, 2, 3).reshape(1, cores, req_count * piece, width)
        return moved

    def across(total, shift):
        return lax.ppermute(total, "hx", [(i, (i + shift) % sides) for i in range(sides)])

    others = [(request, shift) for shift in range(1, sides) for request in range(local)]
    wait, moves = (), []
    for request, shift in others:
        rows, _ = attended(request, shift, wait)
        wait = (rows,)
        moves.append(move(rows))
    arrived, own = [], []
    for index, (_, shift) in enumerate(others):
        if index < local:
            rows, partial = attended(index, 0, wait, moves[index])
            wait = (rows,)
            own.append(move(after(rows, *arrived) if index == local - 1 else rows))
        else:
            _, partial = attended(0, 0, wait, moves[index])
        arrived.append(across(partial, shift))
    return tuple(
        finish(chunks[0][1], own, weights, arrived, req_count, residual, norm_gain)
    )


def solution(mesh):
    req_count, head_count = mesh.shape["req"], mesh.shape["head"]
    split = Mesh(mesh.devices.reshape(req_count, head_count // 2, 2), ("req", "hx", "hc"))
    heads = ("hx", "hc")
    by_head = P("req", None, heads)
    stream = P(("req", "hx", "hc"), None, None)
    return jax.shard_map(
        body,
        mesh=split,
        in_specs=(by_head,) * 5 + (P("req"), P(heads, None), stream, P()),
        out_specs=(stream, stream),
        check_vma=False,
    )
```

```python
import functools
import math

import jax
import jax.numpy as jnp
from jax import lax
from jax.experimental import pallas as pl
from jax.experimental.pallas import tpu as pltpu
from jax.sharding import Mesh, PartitionSpec as P

QUERY_HEADS = 32
KEY_VALUE_HEADS = 8
HEAD_SIZE = 128
MEMBERS = QUERY_HEADS // KEY_VALUE_HEADS
NEGATIVE_FILLER = -1e30
EXPONENT_SCALE = math.log2(math.e) / math.sqrt(HEAD_SIZE)
CONTRACT_LAST = (((1,), (1,)), ((), ()))
MIB = 2**20


def in_hbm(array):
    return pltpu.with_memory_space_constraint(array, pltpu.HBM)


def resident(array):
    return pltpu.with_memory_space_constraint(array, pltpu.VMEM)


def with_ones(values):
    return jnp.concatenate([values, jnp.ones((values.shape[0], HEAD_SIZE), jnp.bfloat16)], axis=1)


def weights_of(scores, row_max):
    tiled = jnp.concatenate([row_max] * (scores.shape[1] // HEAD_SIZE), axis=1)
    return jnp.exp2((scores - tiled) * EXPONENT_SCALE).astype(jnp.bfloat16)


class Projection:
    def __init__(self, sources, parts, weights, scratch):
        self.sources = sources
        self.weights = weights
        self.parts_ref, self.lhs_ref, self.w_ref, self.parts_sem, self.w_sem = scratch
        core = lax.axis_index("hc")
        self.part_copies = [
            pltpu.make_async_copy(
                part.at[:, core if k == 0 else 1 - core],
                self.parts_ref.at[k, n],
                self.parts_sem.at[k, n],
            )
            for k in range(2)
            for n, part in enumerate(parts)
        ]

    @staticmethod
    def scratch(count, part, weight):
        sources, _, rows, depth = part.shape
        columns = weight.shape[1]
        block = min(512, columns)
        return [
            pltpu.VMEM((2, count, sources, rows, depth), jnp.bfloat16),
            pltpu.VMEM((2, count * sources * rows, depth), jnp.bfloat16),
            pltpu.VMEM((2, columns // block, depth, block), jnp.bfloat16),
            pltpu.SemaphoreType.DMA((2, count)),
            pltpu.SemaphoreType.DMA((2, columns // block)),
        ]

    def weight_copy(self, k, n):
        block = self.w_ref.shape[3]
        return pltpu.make_async_copy(
            self.weights[k].at[:, pl.ds(n * block, block)],
            self.w_ref.at[k, n],
            self.w_sem.at[k, n],
        )

    def start_parts(self):
        for copy in self.part_copies:
            copy.start()

    def start_block(self, n):
        if n < self.w_ref.shape[1]:
            for k in range(2):
                self.weight_copy(k, n).start()

    def arrange(self):
        _, count, sources, rows, depth = self.parts_ref.shape
        size = sources * rows
        target = lax.broadcasted_iota(jnp.int32, (size, size), 0)
        origin = lax.broadcasted_iota(jnp.int32, (size, size), 1)
        wanted = target % self.sources * (size // self.sources) + target // self.sources
        order = jnp.where(origin == wanted, 1.0, 0.0).astype(jnp.bfloat16)
        for copy in self.part_copies:
            copy.wait()
        for k in range(2):
            for n in range(count):
                self.lhs_ref[k, n * size : (n + 1) * size] = jnp.dot(
                    order,
                    self.parts_ref[k, n].reshape(size, depth),
                    preferred_element_type=jnp.float32,
                ).astype(jnp.bfloat16)

    def column_block(self, n):
        for k in range(2):
            self.weight_copy(k, n).wait()
        return jnp.dot(
            self.lhs_ref[0], self.w_ref[0, n], preferred_element_type=jnp.float32
        ) + jnp.dot(self.lhs_ref[1], self.w_ref[1, n], preferred_element_type=jnp.float32)


def attention_kernel(
    request, shift, sides, span, stride, sources, lengths_ref, q_hbm, nk_hbm, nv_hbm, ck_hbm, cv_hbm, *refs
):
    projecting = len(refs) > 12
    if projecting:
        parts_any, w_mine_hbm, w_other_hbm, out_hbm, partial_hbm, *refs = refs
    else:
        out_hbm, *refs = refs
    q_ref, nk_ref, nv_ref, ck_ref, cv_ref, max_ref, acc_ref, done_ref = refs[:8]
    new_sem, cache_sem, out_sem = refs[8:11]
    kv_local, rows = nk_ref.shape[1] // HEAD_SIZE, max_ref.shape[1]
    new_count, slots = nk_ref.shape[0], ck_ref.shape[0]
    small = min(512, slots)
    length = lengths_ref[request]
    side = lax.rem(lax.axis_index("hx") + shift, sides)
    first = side * span
    side_in_queries = side if q_hbm.shape[2] == sides else 0

    new_copies = [
        pltpu.make_async_copy(
            q_hbm.at[request, :, side_in_queries], q_ref, new_sem.at[0]
        ),
        pltpu.make_async_copy(nk_hbm.at[request], nk_ref, new_sem.at[1]),
        pltpu.make_async_copy(nv_hbm.at[request], nv_ref, new_sem.at[2]),
    ]

    def cache_copies(block):
        part = pl.ds(pl.multiple_of(block * small, small), small)
        return (
            pltpu.make_async_copy(
                ck_hbm.at[request, part], ck_ref.at[part], cache_sem.at[0, block]
            ),
            pltpu.make_async_copy(
                cv_hbm.at[request, part], cv_ref.at[part], cache_sem.at[1, block]
            ),
        )

    for copy in new_copies:
        copy.start()
    for block in range(slots // small):

        @pl.when(block * small < length)
        def _(block=block):
            for copy in cache_copies(block):
                copy.start()

    def absorb(g, keys, values, mask, fresh):
        def product(h):
            low = (g * MEMBERS + h) * HEAD_SIZE
            return lax.dot_general(
                q_ref[:, :, low : low + HEAD_SIZE].reshape(rows, HEAD_SIZE),
                keys,
                CONTRACT_LAST,
                preferred_element_type=jnp.float32,
            )

        scores = product(0)
        for h in range(MEMBERS):
            index = g * MEMBERS + h
            following = product(h + 1) if h + 1 < MEMBERS else None
            if mask is not None:
                scores = jnp.where(mask, scores, NEGATIVE_FILLER)
            block_max = jnp.max(scores, axis=1, keepdims=True)
            if fresh:
                new_max = jnp.broadcast_to(block_max, (rows, HEAD_SIZE))
                weights = weights_of(scores, new_max)
                acc_ref[index] = jnp.dot(weights, values, preferred_element_type=jnp.float32)
            else:
                old_max = max_ref[index]
                new_max = jnp.maximum(old_max, block_max)
                rescale = jnp.exp2((old_max - new_max) * EXPONENT_SCALE)
                weights = weights_of(scores, new_max)
                acc_ref[index] = acc_ref[index] * jnp.concatenate(
                    [rescale, rescale], axis=1
                ) + jnp.dot(weights, values, preferred_element_type=jnp.float32)
            max_ref[index] = new_max
            scores = following

    for copy in new_copies:
        copy.wait()
    if projecting:
        stage_ref, stage_sem = refs[11:13]
        projection = Projection(sources, [parts_any], (w_mine_hbm, w_other_hbm), refs[13:])
        projection.start_parts()
        for n in range(projection.w_ref.shape[1]):
            projection.start_block(n)
    row = lax.broadcasted_iota(jnp.int32, (rows, 1), 0)
    position = row // span * stride + first + row % span
    visible = lax.broadcasted_iota(jnp.int32, (rows, new_count), 1) <= position
    for g in range(kv_local):
        lanes = slice(g * HEAD_SIZE, (g + 1) * HEAD_SIZE)
        absorb(g, nk_ref[:, lanes], with_ones(nv_ref[:, lanes]), visible, True)

    def cache_block(start, extent, masked):
        for block in range(extent // small):
            for copy in cache_copies(start // small + block):
                copy.wait()
        mask = None
        if masked:
            mask = lax.broadcasted_iota(jnp.int32, (1, extent), 1) < length - start
        for g in range(kv_local):
            lanes = slice(g * HEAD_SIZE, (g + 1) * HEAD_SIZE)
            absorb(
                g,
                ck_ref[pl.ds(start, extent), lanes],
                with_ones(cv_ref[pl.ds(start, extent), lanes]),
                mask,
                False,
            )

    start, extent = jnp.int32(0), slots
    while extent >= small:
        fits = length - start >= extent

        @pl.when(fits)
        def _(start=start, extent=extent):
            cache_block(pl.multiple_of(start, small), extent, False)

        start = jnp.where(fits, start + extent, start)
        extent //= 2

    @pl.when(start < length)
    def _():
        cache_block(pl.multiple_of(start, small), small, True)

    group = MEMBERS * HEAD_SIZE
    out_copies = []
    for g in range(kv_local):
        for index in range(g * MEMBERS, (g + 1) * MEMBERS):
            total = acc_ref[index]
            done_ref[:, index * HEAD_SIZE : (index + 1) * HEAD_SIZE] = (
                total[:, :HEAD_SIZE] / total[:, HEAD_SIZE:]
            ).astype(jnp.bfloat16)
        lanes = pl.ds(g * group, group)
        out_copies.append(
            pltpu.make_async_copy(done_ref.at[:, lanes], out_hbm.at[:, lanes], out_sem.at[g])
        )
        out_copies[-1].start()
    if projecting:
        projection.arrange()
        block = projection.w_ref.shape[3]
        for n in range(projection.w_ref.shape[1]):
            lanes = pl.ds(n * block, block)
            stage_ref[:, n * block : (n + 1) * block] = projection.column_block(n).astype(
                jnp.bfloat16
            )
            out_copies.append(
                pltpu.make_async_copy(
                    stage_ref.at[:, lanes], partial_hbm.at[:, lanes], stage_sem.at[n]
                )
            )
            out_copies[-1].start()
    for copy in out_copies:
        copy.wait()


def attend(request, shift, sides, span, stride, sources, lengths, q, nk, nv, ck, cv, moved=None, weights=()):
    _, blocks, _, q_span, width = q.shape
    rows = blocks * q_span
    new_count, slots, kv_width = nk.shape[1], ck.shape[1], nk.shape[2]
    small = min(512, slots)
    in_place = pl.BlockSpec(memory_space=pltpu.HBM)
    out_specs = [in_place]
    out_shape = [pltpu.HBM((rows, width), jnp.bfloat16)]
    heads = width // HEAD_SIZE
    scratch = [
        pltpu.VMEM((blocks, q_span, width), jnp.bfloat16),
        pltpu.VMEM((new_count, kv_width), jnp.bfloat16),
        pltpu.VMEM((new_count, kv_width), jnp.bfloat16),
        pltpu.VMEM((slots, kv_width), jnp.bfloat16),
        pltpu.VMEM((slots, kv_width), jnp.bfloat16),
        pltpu.VMEM((heads, rows, HEAD_SIZE), jnp.float32),
        pltpu.VMEM((heads, rows, 2 * HEAD_SIZE), jnp.float32),
        pltpu.VMEM((rows, width), jnp.bfloat16),
        pltpu.SemaphoreType.DMA((3,)),
        pltpu.SemaphoreType.DMA((2, slots // small)),
        pltpu.SemaphoreType.DMA((kv_width // HEAD_SIZE,)),
    ]
    operands = [in_hbm(a) for a in (q, nk, nv, ck, cv)]
    if moved is not None:
        columns = weights[0].shape[1]
        out_rows = moved.shape[0] * moved.shape[2]
        operands += [in_hbm(moved)] + [in_hbm(w) for w in weights]
        out_specs.append(in_place)
        out_shape.append(pltpu.HBM((out_rows, columns), jnp.bfloat16))
        projection = Projection.scratch(1, moved, weights[0])
        scratch.append(pltpu.VMEM((out_rows, columns), jnp.bfloat16))
        scratch.append(pltpu.SemaphoreType.DMA((projection[2].shape[1],)))
        scratch += projection
    out = pl.pallas_call(
        functools.partial(attention_kernel, request, shift, sides, span, stride, sources),
        in_specs=[pl.BlockSpec(memory_space=pltpu.SMEM)] + [in_place] * len(operands),
        out_specs=out_specs,
        scratch_shapes=scratch,
        out_shape=out_shape,
        compiler_params=pltpu.CompilerParams(vmem_limit_bytes=48 * MIB),
        name="attend",
    )(lengths, *operands)
    return out if moved is not None else (out[0], None)


def projection_kernel(sources, part_hbm, w_mine_hbm, w_other_hbm, out_hbm, *refs):
    stage_ref, stage_sem = refs[:2]
    projection = Projection(sources, [part_hbm], (w_mine_hbm, w_other_hbm), refs[2:])
    blocks, block = projection.w_ref.shape[1], projection.w_ref.shape[3]
    ahead = 3
    projection.start_parts()
    for n in range(ahead):
        projection.start_block(n)
    projection.arrange()
    out_copies = []
    for n in range(blocks):
        projection.start_block(n + ahead)
        lanes = pl.ds(n * block, block)
        stage_ref[:, n * block : (n + 1) * block] = projection.column_block(n).astype(jnp.bfloat16)
        out_copies.append(
            pltpu.make_async_copy(stage_ref.at[:, lanes], out_hbm.at[:, lanes], stage_sem.at[n])
        )
        out_copies[-1].start()
    for copy in out_copies:
        copy.wait()


def project(moved, weights, sources):
    columns = weights[0].shape[1]
    rows = moved.shape[0] * moved.shape[2]
    in_place = pl.BlockSpec(memory_space=pltpu.HBM)
    scratch = Projection.scratch(1, moved, weights[0])
    return pl.pallas_call(
        functools.partial(projection_kernel, sources),
        in_specs=[in_place] * 3,
        out_specs=in_place,
        scratch_shapes=[
            pltpu.VMEM((rows, columns), jnp.bfloat16),
            pltpu.SemaphoreType.DMA((scratch[2].shape[1],)),
        ]
        + scratch,
        out_shape=pltpu.HBM((rows, columns), jnp.bfloat16),
        compiler_params=pltpu.CompilerParams(vmem_limit_bytes=32 * MIB),
        name="project",
    )(in_hbm(moved), *[in_hbm(w) for w in weights])


def final_kernel(groups, sources, *refs):
    count = sum(groups)
    parts_any, refs = refs[:count], refs[count:]
    moved_any, w_mine_hbm, w_other_hbm, residual_hbm, gain_ref, hidden_hbm, normed_hbm, *refs = refs
    parts_ref, residual_ref, hidden_ref, normed_ref, rows_ref, square_ref = refs[:6]
    parts_sem, residual_sem, hidden_sem, normed_sem = refs[6:10]
    projection = Projection(sources, [moved_any], (w_mine_hbm, w_other_hbm), refs[10:])
    blocks, pieces, requests, block = residual_ref.shape
    rows, local = pieces * requests, len(groups)
    each = rows // local
    strips = block // HEAD_SIZE

    def lanes(n):
        return pl.ds(n * block, block)

    def block_copies(n):
        copies = [
            pltpu.make_async_copy(
                residual_hbm.at[:, :, lanes(n)], residual_ref.at[n], residual_sem.at[n]
            )
        ]
        for index, part in enumerate(parts_any):
            copies.append(
                pltpu.make_async_copy(
                    part.at[:, lanes(n)], parts_ref.at[index, n], parts_sem.at[index, n]
                )
            )
        return copies

    def start_block(n):
        projection.start_block(n)
        if n < blocks:
            for copy in block_copies(n):
                copy.start()

    ahead = 3
    projection.start_parts()
    for n in range(ahead):
        start_block(n)
    projection.arrange()
    out_copies = []
    square_ref[...] = jnp.zeros_like(square_ref)
    for n in range(blocks):
        start_block(n + ahead)
        own = projection.column_block(n)
        for copy in block_copies(n):
            copy.wait()
        taken = 0
        for request, size in enumerate(groups):
            total = parts_ref[taken, n].astype(jnp.float32)
            for index in range(taken + 1, taken + size):
                total += parts_ref[index, n].astype(jnp.float32)
            taken += size
            if request == local - 1:
                total += own
            for p in range(strips):
                rows_ref[n * strips + p, pl.ds(request, each, stride=local), :] = total[
                    :, p * HEAD_SIZE : (p + 1) * HEAD_SIZE
                ]
        square = square_ref[...]
        for p in range(strips):
            span = slice(p * HEAD_SIZE, (p + 1) * HEAD_SIZE)
            value = rows_ref[n * strips + p] + residual_ref[n, :, :, span].reshape(
                rows, HEAD_SIZE
            ).astype(jnp.float32)
            hidden_ref[n, :, :, span] = value.reshape(pieces, requests, HEAD_SIZE).astype(
                jnp.bfloat16
            )
            rows_ref[n * strips + p] = value
            square += value * value
        square_ref[...] = square
        out_copies.append(
            pltpu.make_async_copy(
                hidden_ref.at[n], hidden_hbm.at[:, :, lanes(n)], hidden_sem.at[n]
            )
        )
        out_copies[-1].start()
    mean = jnp.sum(square_ref[...], axis=1, keepdims=True) * (1.0 / (blocks * block))
    scale = jnp.broadcast_to(lax.rsqrt(mean + 1e-05), (rows, HEAD_SIZE))
    for n in range(blocks):
        for p in range(strips):
            span = slice(p * HEAD_SIZE, (p + 1) * HEAD_SIZE)
            low = n * block + p * HEAD_SIZE
            gain = gain_ref[:, low : low + HEAD_SIZE].astype(jnp.float32)
            normed_ref[n, :, :, span] = (
                (rows_ref[n * strips + p] * scale * gain)
                .reshape(pieces, requests, HEAD_SIZE)
                .astype(jnp.bfloat16)
            )
        out_copies.append(
            pltpu.make_async_copy(
                normed_ref.at[n], normed_hbm.at[:, :, lanes(n)], normed_sem.at[n]
            )
        )
        out_copies[-1].start()
    for copy in out_copies:
        copy.wait()


def finish(groups, moved, weights, sources, residual, gain):
    pieces, requests, columns = residual.shape
    rows = pieces * requests
    block = min(512, columns)
    count = columns // block
    flat = [part for group in groups for part in group]
    in_place = pl.BlockSpec(memory_space=pltpu.HBM)
    shape = pltpu.HBM(residual.shape, jnp.bfloat16)
    stream = pltpu.VMEM((count, pieces, requests, block), jnp.bfloat16)
    return pl.pallas_call(
        functools.partial(final_kernel, tuple(len(group) for group in groups), sources),
        in_specs=[pl.BlockSpec(memory_space=pl.ANY)] * (len(flat) + 1)
        + [in_place] * 3
        + [pl.BlockSpec(memory_space=pltpu.VMEM)],
        out_specs=[in_place, in_place],
        scratch_shapes=[
            pltpu.VMEM((len(flat), count, rows // len(groups), block), jnp.bfloat16),
            stream,
            stream,
            stream,
            pltpu.VMEM((columns // HEAD_SIZE, rows, HEAD_SIZE), jnp.float32),
            pltpu.VMEM((rows, HEAD_SIZE), jnp.float32),
            pltpu.SemaphoreType.DMA((len(flat), count)),
            pltpu.SemaphoreType.DMA((count,)),
            pltpu.SemaphoreType.DMA((count,)),
            pltpu.SemaphoreType.DMA((count,)),
        ]
        + Projection.scratch(1, moved, weights[0]),
        out_shape=[shape, shape],
        compiler_params=pltpu.CompilerParams(vmem_limit_bytes=48 * MIB),
        name="finish",
    )(
        *[in_hbm(part) for part in flat[:-1]],
        flat[-1],
        moved,
        *[in_hbm(w) for w in weights],
        in_hbm(residual),
        gain.reshape(1, columns),
    )


def after(array, *others):
    return lax.optimization_barrier((array,) + others)[0] if others else array


def body(
    queries,
    new_keys,
    incoming_values,
    request_cached_keys,
    request_cached_values,
    cache_lengths,
    out_weight,
    residual,
    norm_gain,
):
    local, new_count, width = queries.shape
    req_count, sides, cores = (lax.axis_size(a) for a in ("req", "hx", "hc"))
    piece = new_count // (req_count * sides * cores)
    span, stride = cores * piece, sides * cores * piece
    whole_tiles = piece % 16 == 0
    by_side = queries.reshape(local, req_count, sides, span, width)

    def queries_of(shift):
        if whole_tiles:
            return by_side
        side = lax.rem(lax.axis_index("hx") + shift, sides)
        q = lax.dynamic_index_in_dim(by_side, side, 2, keepdims=False)
        return q.reshape(local, 1, 1, req_count * span, width)

    def attended(request, shift, wait, moved=None, weights=()):
        return attend(
            request,
            shift,
            sides,
            span,
            stride,
            req_count,
            after(cache_lengths, *wait),
            queries_of(shift),
            new_keys,
            incoming_values,
            request_cached_keys,
            request_cached_values,
            moved,
            weights,
        )

    def move(rows):
        moved = lax.all_to_all(rows, ("req", "hc"), 0, 0, tiled=True)
        moved = moved.reshape(req_count, cores, piece, width)
        if not whole_tiles:
            moved = moved.transpose(1, 0, 2, 3).reshape(1, cores, req_count * piece, width)
        return moved

    def across(total, shift):
        return lax.ppermute(total, "hx", [(i, (i + shift) % sides) for i in range(sides)])

    others = [(request, shift) for shift in range(1, sides) for request in range(local)]
    wait, moves, weights = (), [], None
    for request, shift in others:
        rows, _ = attended(request, shift, wait)
        wait = (rows,)
        moves.append(move(rows))
        if weights is None:
            sibling = lax.ppermute(after(out_weight, rows), "hc", [(0, 1), (1, 0)])
            weights = (out_weight, sibling)
    groups, own = [[] for _ in range(local)], []
    for index, (request, shift) in enumerate(others):
        if index < local:
            rows, partial = attended(index, 0, wait, moves[index], weights)
            hold = [part for group in groups for part in group] if index == local - 1 else ()
            wait = (rows,)
            own.append(move(after(rows, *hold)))
        else:
            partial = project(after(moves[index], *wait), weights, req_count)
        groups[request].append(across(partial, shift))
    for request in range(local - 1):
        groups[request].append(project(after(own[request], *wait), weights, req_count))
        wait = (groups[request][-1],)
    return tuple(finish(groups, own[-1], weights, req_count, residual, norm_gain))


def solution(mesh):
    req_count, head_count = mesh.shape["req"], mesh.shape["head"]
    split = Mesh(mesh.devices.reshape(req_count, head_count // 2, 2), ("req", "hx", "hc"))
    heads = ("hx", "hc")
    by_head = P("req", None, heads)
    stream = P(("req", "hx", "hc"), None, None)
    return jax.shard_map(
        body,
        mesh=split,
        in_specs=(by_head,) * 5 + (P("req"), P(heads, None), stream, P()),
        out_specs=(stream, stream),
        check_vma=False,
    )
```

```python
import functools
import math

import jax
import jax.numpy as jnp
from jax import lax
from jax.experimental import pallas as pl
from jax.experimental.pallas import tpu as pltpu
from jax.sharding import Mesh, PartitionSpec as P

QUERY_HEADS = 32
KEY_VALUE_HEADS = 8
HEAD_SIZE = 128
MEMBERS = QUERY_HEADS // KEY_VALUE_HEADS
NEGATIVE_FILLER = -1e30
EXPONENT_SCALE = math.log2(math.e) / math.sqrt(HEAD_SIZE)
CONTRACT_LAST = (((1,), (1,)), ((), ()))
MIB = 2**20


def in_hbm(array):
    return pltpu.with_memory_space_constraint(array, pltpu.HBM)


def resident(array):
    return pltpu.with_memory_space_constraint(array, pltpu.VMEM)


def with_ones(values):
    return jnp.concatenate([values, jnp.ones((values.shape[0], HEAD_SIZE), jnp.bfloat16)], axis=1)


def weights_of(scores, row_max):
    tiled = jnp.concatenate([row_max] * (scores.shape[1] // HEAD_SIZE), axis=1)
    return jnp.exp2((scores - tiled) * EXPONENT_SCALE).astype(jnp.bfloat16)


class Projection:
    def __init__(self, sources, parts, weights, scratch):
        self.sources = sources
        self.weights = weights
        self.parts_ref, self.lhs_ref, self.w_ref, self.parts_sem, self.w_sem = scratch
        core = lax.axis_index("hc")
        self.part_copies = [
            pltpu.make_async_copy(
                part.at[:, core if k == 0 else 1 - core],
                self.parts_ref.at[k, n],
                self.parts_sem.at[k, n],
            )
            for k in range(2)
            for n, part in enumerate(parts)
        ]

    @staticmethod
    def scratch(count, part, weight):
        sources, _, rows, depth = part.shape
        columns = weight.shape[1]
        block = min(512, columns)
        return [
            pltpu.VMEM((2, count, sources, rows, depth), jnp.bfloat16),
            pltpu.VMEM((2, count * sources * rows, depth), jnp.bfloat16),
            pltpu.VMEM((2, columns // block, depth, block), jnp.bfloat16),
            pltpu.SemaphoreType.DMA((2, count)),
            pltpu.SemaphoreType.DMA((2, columns // block)),
        ]

    def weight_copy(self, k, n):
        block = self.w_ref.shape[3]
        return pltpu.make_async_copy(
            self.weights[k].at[:, pl.ds(n * block, block)],
            self.w_ref.at[k, n],
            self.w_sem.at[k, n],
        )

    def start_parts(self):
        for copy in self.part_copies:
            copy.start()

    def start_block(self, n):
        if n < self.w_ref.shape[1]:
            for k in range(2):
                self.weight_copy(k, n).start()

    def arrange(self):
        _, count, sources, rows, depth = self.parts_ref.shape
        size = sources * rows
        target = lax.broadcasted_iota(jnp.int32, (size, size), 0)
        origin = lax.broadcasted_iota(jnp.int32, (size, size), 1)
        wanted = target % self.sources * (size // self.sources) + target // self.sources
        order = jnp.where(origin == wanted, 1.0, 0.0).astype(jnp.bfloat16)
        for copy in self.part_copies:
            copy.wait()
        for k in range(2):
            for n in range(count):
                self.lhs_ref[k, n * size : (n + 1) * size] = jnp.dot(
                    order,
                    self.parts_ref[k, n].reshape(size, depth),
                    preferred_element_type=jnp.float32,
                ).astype(jnp.bfloat16)

    def column_block(self, n):
        for k in range(2):
            self.weight_copy(k, n).wait()
        return jnp.dot(
            self.lhs_ref[0], self.w_ref[0, n], preferred_element_type=jnp.float32
        ) + jnp.dot(self.lhs_ref[1], self.w_ref[1, n], preferred_element_type=jnp.float32)


def attention_kernel(
    request, shift, sides, span, stride, sources, lengths_ref, q_hbm, nk_hbm, nv_hbm, ck_hbm, cv_hbm, *refs
):
    projecting = len(refs) > 12
    if projecting:
        parts_any, w_mine_hbm, w_other_hbm, out_hbm, partial_hbm, *refs = refs
    else:
        out_hbm, *refs = refs
    q_ref, nk_ref, nv_ref, ck_ref, cv_ref, max_ref, acc_ref, done_ref = refs[:8]
    new_sem, cache_sem, out_sem = refs[8:11]
    kv_local, rows = nk_ref.shape[1] // HEAD_SIZE, max_ref.shape[1]
    new_count, slots = nk_ref.shape[0], ck_ref.shape[0]
    small = min(512, slots)
    length = lengths_ref[request]
    side = lax.rem(lax.axis_index("hx") + shift, sides)
    first = side * span
    side_in_queries = side if q_hbm.shape[2] == sides else 0

    new_copies = [
        pltpu.make_async_copy(
            q_hbm.at[request, :, side_in_queries], q_ref, new_sem.at[0]
        ),
        pltpu.make_async_copy(nk_hbm.at[request], nk_ref, new_sem.at[1]),
        pltpu.make_async_copy(nv_hbm.at[request], nv_ref, new_sem.at[2]),
    ]

    def cache_copies(block):
        part = pl.ds(pl.multiple_of(block * small, small), small)
        return (
            pltpu.make_async_copy(
                ck_hbm.at[request, part], ck_ref.at[part], cache_sem.at[0, block]
            ),
            pltpu.make_async_copy(
                cv_hbm.at[request, part], cv_ref.at[part], cache_sem.at[1, block]
            ),
        )

    for copy in new_copies:
        copy.start()
    for block in range(slots // small):

        @pl.when(block * small < length)
        def _(block=block):
            for copy in cache_copies(block):
                copy.start()

    def absorb(g, keys, values, mask, fresh):
        def product(h):
            low = (g * MEMBERS + h) * HEAD_SIZE
            return lax.dot_general(
                q_ref[:, :, low : low + HEAD_SIZE].reshape(rows, HEAD_SIZE),
                keys,
                CONTRACT_LAST,
                preferred_element_type=jnp.float32,
            )

        scores = product(0)
        for h in range(MEMBERS):
            index = g * MEMBERS + h
            following = product(h + 1) if h + 1 < MEMBERS else None
            if mask is not None:
                scores = jnp.where(mask, scores, NEGATIVE_FILLER)
            block_max = jnp.max(scores, axis=1, keepdims=True)
            if fresh:
                new_max = jnp.broadcast_to(block_max, (rows, HEAD_SIZE))
                weights = weights_of(scores, new_max)
                acc_ref[index] = jnp.dot(weights, values, preferred_element_type=jnp.float32)
            else:
                old_max = max_ref[index]
                new_max = jnp.maximum(old_max, block_max)
                rescale = jnp.exp2((old_max - new_max) * EXPONENT_SCALE)
                weights = weights_of(scores, new_max)
                acc_ref[index] = acc_ref[index] * jnp.concatenate(
                    [rescale, rescale], axis=1
                ) + jnp.dot(weights, values, preferred_element_type=jnp.float32)
            max_ref[index] = new_max
            scores = following

    for copy in new_copies:
        copy.wait()
    if projecting:
        stage_ref, stage_sem = refs[11:13]
        projection = Projection(sources, [parts_any], (w_mine_hbm, w_other_hbm), refs[13:])
        projection.start_parts()
        for n in range(projection.w_ref.shape[1]):
            projection.start_block(n)
    row = lax.broadcasted_iota(jnp.int32, (rows, 1), 0)
    position = row // span * stride + first + row % span
    visible = lax.broadcasted_iota(jnp.int32, (rows, new_count), 1) <= position
    for g in range(kv_local):
        lanes = slice(g * HEAD_SIZE, (g + 1) * HEAD_SIZE)
        absorb(g, nk_ref[:, lanes], with_ones(nv_ref[:, lanes]), visible, True)

    def cache_block(start, extent, masked):
        for block in range(extent // small):
            for copy in cache_copies(start // small + block):
                copy.wait()
        mask = None
        if masked:
            mask = lax.broadcasted_iota(jnp.int32, (1, extent), 1) < length - start
        for g in range(kv_local):
            lanes = slice(g * HEAD_SIZE, (g + 1) * HEAD_SIZE)
            absorb(
                g,
                ck_ref[pl.ds(start, extent), lanes],
                with_ones(cv_ref[pl.ds(start, extent), lanes]),
                mask,
                False,
            )

    start, extent = jnp.int32(0), slots
    while extent >= small:
        fits = length - start >= extent

        @pl.when(fits)
        def _(start=start, extent=extent):
            cache_block(pl.multiple_of(start, small), extent, False)

        start = jnp.where(fits, start + extent, start)
        extent //= 2

    @pl.when(start < length)
    def _():
        cache_block(pl.multiple_of(start, small), small, True)

    group = MEMBERS * HEAD_SIZE
    out_copies = []
    for g in range(kv_local):
        for index in range(g * MEMBERS, (g + 1) * MEMBERS):
            total = acc_ref[index]
            done_ref[:, index * HEAD_SIZE : (index + 1) * HEAD_SIZE] = (
                total[:, :HEAD_SIZE] / total[:, HEAD_SIZE:]
            ).astype(jnp.bfloat16)
        lanes = pl.ds(g * group, group)
        out_copies.append(
            pltpu.make_async_copy(done_ref.at[:, lanes], out_hbm.at[:, lanes], out_sem.at[g])
        )
        out_copies[-1].start()
    if projecting:
        projection.arrange()
        block = projection.w_ref.shape[3]
        for n in range(projection.w_ref.shape[1]):
            lanes = pl.ds(n * block, block)
            stage_ref[:, n * block : (n + 1) * block] = projection.column_block(n).astype(
                jnp.bfloat16
            )
            out_copies.append(
                pltpu.make_async_copy(
                    stage_ref.at[:, lanes], partial_hbm.at[:, lanes], stage_sem.at[n]
                )
            )
            out_copies[-1].start()
    for copy in out_copies:
        copy.wait()


def attend(request, shift, sides, span, stride, sources, lengths, q, nk, nv, ck, cv, moved=None, weights=()):
    _, blocks, _, q_span, width = q.shape
    rows = blocks * q_span
    new_count, slots, kv_width = nk.shape[1], ck.shape[1], nk.shape[2]
    small = min(512, slots)
    in_place = pl.BlockSpec(memory_space=pltpu.HBM)
    out_specs = [in_place]
    out_shape = [pltpu.HBM((rows, width), jnp.bfloat16)]
    heads = width // HEAD_SIZE
    scratch = [
        pltpu.VMEM((blocks, q_span, width), jnp.bfloat16),
        pltpu.VMEM((new_count, kv_width), jnp.bfloat16),
        pltpu.VMEM((new_count, kv_width), jnp.bfloat16),
        pltpu.VMEM((slots, kv_width), jnp.bfloat16),
        pltpu.VMEM((slots, kv_width), jnp.bfloat16),
        pltpu.VMEM((heads, rows, HEAD_SIZE), jnp.float32),
        pltpu.VMEM((heads, rows, 2 * HEAD_SIZE), jnp.float32),
        pltpu.VMEM((rows, width), jnp.bfloat16),
        pltpu.SemaphoreType.DMA((3,)),
        pltpu.SemaphoreType.DMA((2, slots // small)),
        pltpu.SemaphoreType.DMA((kv_width // HEAD_SIZE,)),
    ]
    operands = [in_hbm(a) for a in (q, nk, nv, ck, cv)]
    if moved is not None:
        columns = weights[0].shape[1]
        out_rows = moved.shape[0] * moved.shape[2]
        operands += [in_hbm(moved)] + [in_hbm(w) for w in weights]
        out_specs.append(in_place)
        out_shape.append(pltpu.HBM((out_rows, columns), jnp.bfloat16))
        projection = Projection.scratch(1, moved, weights[0])
        scratch.append(pltpu.VMEM((out_rows, columns), jnp.bfloat16))
        scratch.append(pltpu.SemaphoreType.DMA((projection[2].shape[1],)))
        scratch += projection
    out = pl.pallas_call(
        functools.partial(attention_kernel, request, shift, sides, span, stride, sources),
        in_specs=[pl.BlockSpec(memory_space=pltpu.SMEM)] + [in_place] * len(operands),
        out_specs=out_specs,
        scratch_shapes=scratch,
        out_shape=out_shape,
        compiler_params=pltpu.CompilerParams(vmem_limit_bytes=48 * MIB),
        name="attend",
    )(in_hbm(lengths), *operands)
    return out if moved is not None else (out[0], None)


def projection_kernel(sources, part_hbm, w_mine_hbm, w_other_hbm, out_hbm, *refs):
    stage_ref, stage_sem = refs[:2]
    projection = Projection(sources, [part_hbm], (w_mine_hbm, w_other_hbm), refs[2:])
    blocks, block = projection.w_ref.shape[1], projection.w_ref.shape[3]
    ahead = 3
    projection.start_parts()
    for n in range(ahead):
        projection.start_block(n)
    projection.arrange()
    out_copies = []
    for n in range(blocks):
        projection.start_block(n + ahead)
        lanes = pl.ds(n * block, block)
        stage_ref[:, n * block : (n + 1) * block] = projection.column_block(n).astype(jnp.bfloat16)
        out_copies.append(
            pltpu.make_async_copy(stage_ref.at[:, lanes], out_hbm.at[:, lanes], stage_sem.at[n])
        )
        out_copies[-1].start()
    for copy in out_copies:
        copy.wait()


def project(moved, weights, sources):
    columns = weights[0].shape[1]
    rows = moved.shape[0] * moved.shape[2]
    in_place = pl.BlockSpec(memory_space=pltpu.HBM)
    scratch = Projection.scratch(1, moved, weights[0])
    return pl.pallas_call(
        functools.partial(projection_kernel, sources),
        in_specs=[in_place] * 3,
        out_specs=in_place,
        scratch_shapes=[
            pltpu.VMEM((rows, columns), jnp.bfloat16),
            pltpu.SemaphoreType.DMA((scratch[2].shape[1],)),
        ]
        + scratch,
        out_shape=pltpu.HBM((rows, columns), jnp.bfloat16),
        compiler_params=pltpu.CompilerParams(vmem_limit_bytes=32 * MIB),
        name="project",
    )(in_hbm(moved), *[in_hbm(w) for w in weights])


def final_kernel(groups, sources, *refs):
    count = sum(groups)
    parts_any, refs = refs[:count], refs[count:]
    moved_any, w_mine_hbm, w_other_hbm, residual_hbm, gain_ref, hidden_hbm, normed_hbm, *refs = refs
    parts_ref, residual_ref, hidden_ref, normed_ref, rows_ref, square_ref = refs[:6]
    parts_sem, residual_sem, hidden_sem, normed_sem = refs[6:10]
    projection = Projection(sources, [moved_any], (w_mine_hbm, w_other_hbm), refs[10:])
    blocks, pieces, requests, block = residual_ref.shape
    rows, local = pieces * requests, len(groups)
    each = rows // local
    strips = block // HEAD_SIZE

    def lanes(n):
        return pl.ds(n * block, block)

    def block_copies(n):
        copies = [
            pltpu.make_async_copy(
                residual_hbm.at[:, :, lanes(n)], residual_ref.at[n], residual_sem.at[n]
            )
        ]
        for index, part in enumerate(parts_any):
            copies.append(
                pltpu.make_async_copy(
                    part.at[:, lanes(n)], parts_ref.at[index, n], parts_sem.at[index, n]
                )
            )
        return copies

    def start_block(n):
        projection.start_block(n)
        if n < blocks:
            for copy in block_copies(n):
                copy.start()

    ahead = 5
    projection.start_parts()
    for n in range(ahead):
        start_block(n)
    projection.arrange()
    out_copies = []
    square_ref[...] = jnp.zeros_like(square_ref)
    for n in range(blocks):
        start_block(n + ahead)
        own = projection.column_block(n)
        for copy in block_copies(n):
            copy.wait()
        taken = 0
        for request, size in enumerate(groups):
            total = parts_ref[taken, n].astype(jnp.float32)
            for index in range(taken + 1, taken + size):
                total += parts_ref[index, n].astype(jnp.float32)
            taken += size
            if request == local - 1:
                total += own
            for p in range(strips):
                rows_ref[n * strips + p, pl.ds(request, each, stride=local), :] = total[
                    :, p * HEAD_SIZE : (p + 1) * HEAD_SIZE
                ]
        square = square_ref[...]
        for p in range(strips):
            span = slice(p * HEAD_SIZE, (p + 1) * HEAD_SIZE)
            value = rows_ref[n * strips + p] + residual_ref[n, :, :, span].reshape(
                rows, HEAD_SIZE
            ).astype(jnp.float32)
            hidden_ref[n, :, :, span] = value.reshape(pieces, requests, HEAD_SIZE).astype(
                jnp.bfloat16
            )
            rows_ref[n * strips + p] = value
            square += value * value
        square_ref[...] = square
        out_copies.append(
            pltpu.make_async_copy(
                hidden_ref.at[n], hidden_hbm.at[:, :, lanes(n)], hidden_sem.at[n]
            )
        )
        out_copies[-1].start()
    mean = jnp.sum(square_ref[...], axis=1, keepdims=True) * (1.0 / (blocks * block))
    scale = jnp.broadcast_to(lax.rsqrt(mean + 1e-05), (rows, HEAD_SIZE))
    for n in range(blocks):
        for p in range(strips):
            span = slice(p * HEAD_SIZE, (p + 1) * HEAD_SIZE)
            low = n * block + p * HEAD_SIZE
            gain = gain_ref[:, low : low + HEAD_SIZE].astype(jnp.float32)
            normed_ref[n, :, :, span] = (
                (rows_ref[n * strips + p] * scale * gain)
                .reshape(pieces, requests, HEAD_SIZE)
                .astype(jnp.bfloat16)
            )
        out_copies.append(
            pltpu.make_async_copy(
                normed_ref.at[n], normed_hbm.at[:, :, lanes(n)], normed_sem.at[n]
            )
        )
        out_copies[-1].start()
    for copy in out_copies:
        copy.wait()


def finish(groups, moved, weights, sources, residual, gain):
    pieces, requests, columns = residual.shape
    rows = pieces * requests
    block = min(512, columns)
    count = columns // block
    flat = [part for group in groups for part in group]
    in_place = pl.BlockSpec(memory_space=pltpu.HBM)
    shape = pltpu.HBM(residual.shape, jnp.bfloat16)
    stream = pltpu.VMEM((count, pieces, requests, block), jnp.bfloat16)
    return pl.pallas_call(
        functools.partial(final_kernel, tuple(len(group) for group in groups), sources),
        in_specs=[pl.BlockSpec(memory_space=pl.ANY)] * (len(flat) + 1)
        + [in_place] * 3
        + [pl.BlockSpec(memory_space=pltpu.VMEM)],
        out_specs=[in_place, in_place],
        scratch_shapes=[
            pltpu.VMEM((len(flat), count, rows // len(groups), block), jnp.bfloat16),
            stream,
            stream,
            stream,
            pltpu.VMEM((columns // HEAD_SIZE, rows, HEAD_SIZE), jnp.float32),
            pltpu.VMEM((rows, HEAD_SIZE), jnp.float32),
            pltpu.SemaphoreType.DMA((len(flat), count)),
            pltpu.SemaphoreType.DMA((count,)),
            pltpu.SemaphoreType.DMA((count,)),
            pltpu.SemaphoreType.DMA((count,)),
        ]
        + Projection.scratch(1, moved, weights[0]),
        out_shape=[shape, shape],
        compiler_params=pltpu.CompilerParams(vmem_limit_bytes=48 * MIB),
        name="finish",
    )(
        *[in_hbm(part) for part in flat[:-1]],
        flat[-1],
        moved,
        *[in_hbm(w) for w in weights],
        in_hbm(residual),
        gain.reshape(1, columns),
    )


def after(array, *others):
    return lax.optimization_barrier((array,) + others)[0] if others else array


def body(
    queries,
    new_keys,
    incoming_values,
    request_cached_keys,
    request_cached_values,
    cache_lengths,
    out_weight,
    residual,
    norm_gain,
):
    local, new_count, width = queries.shape
    req_count, sides, cores = (lax.axis_size(a) for a in ("req", "hx", "hc"))
    piece = new_count // (req_count * sides * cores)
    span, stride = cores * piece, sides * cores * piece
    whole_tiles = piece % 16 == 0
    by_side = queries.reshape(local, req_count, sides, span, width)

    def queries_of(shift):
        if whole_tiles:
            return by_side
        side = lax.rem(lax.axis_index("hx") + shift, sides)
        q = lax.dynamic_index_in_dim(by_side, side, 2, keepdims=False)
        return q.reshape(local, 1, 1, req_count * span, width)

    def attended(request, shift, wait, moved=None, weights=()):
        return attend(
            request,
            shift,
            sides,
            span,
            stride,
            req_count,
            after(cache_lengths, *wait),
            queries_of(shift),
            new_keys,
            incoming_values,
            request_cached_keys,
            request_cached_values,
            moved,
            weights,
        )

    def move(rows):
        moved = lax.all_to_all(rows, ("req", "hc"), 0, 0, tiled=True)
        moved = moved.reshape(req_count, cores, piece, width)
        if not whole_tiles:
            moved = moved.transpose(1, 0, 2, 3).reshape(1, cores, req_count * piece, width)
        return moved

    def across(total, shift):
        return lax.ppermute(total, "hx", [(i, (i + shift) % sides) for i in range(sides)])

    others = [(request, shift) for shift in range(1, sides) for request in range(local)]
    wait, moves, weights = (), [], None
    for request, shift in others:
        rows, _ = attended(request, shift, wait)
        wait = (rows,)
        moves.append(move(rows))
        if weights is None:
            sibling = lax.ppermute(after(out_weight, rows), "hc", [(0, 1), (1, 0)])
            weights = (out_weight, sibling)
    groups, own = [[] for _ in range(local)], []
    for index, (request, shift) in enumerate(others):
        if index < local:
            rows, partial = attended(index, 0, wait, moves[index], weights)
            hold = [part for group in groups for part in group] if index == local - 1 else ()
            wait = (rows,)
            own.append(move(after(rows, *hold)))
        else:
            partial = project(after(moves[index], *wait), weights, req_count)
        groups[request].append(across(partial, shift))
    for request in range(local - 1):
        groups[request].append(project(after(own[request], *wait), weights, req_count))
        wait = (groups[request][-1],)
    return tuple(finish(groups, own[-1], weights, req_count, residual, norm_gain))


def solution(mesh):
    req_count, head_count = mesh.shape["req"], mesh.shape["head"]
    split = Mesh(mesh.devices.reshape(req_count, head_count // 2, 2), ("req", "hx", "hc"))
    heads = ("hx", "hc")
    by_head = P("req", None, heads)
    stream = P(("req", "hx", "hc"), None, None)
    return jax.shard_map(
        body,
        mesh=split,
        in_specs=(by_head,) * 5 + (P("req"), P(heads, None), stream, P()),
        out_specs=(stream, stream),
        check_vma=False,
    )
```
